32 devices in a mesh: groups: 2 (over y), row: 4 (over z), col: 2 (over x), rep: 2 (over core).
Axes of the slice: x: 2, y: 2, z: 4, core: 2. Of those that a mesh axis runs over, the one named last changes fastest.
Arguments:
- tokens: bfloat16 [256, 8192], P(('groups', 'row', 'rep'), 'col'), parts along dimension 0, may hold values from -6 to 6
- gate_blocks: bfloat16 [64, 4, 24, 128, 128], P('col', 'row'), may hold values from -0.09375 to 0.09375
- gate_cols: int32 [64, 4, 24], P('col', 'row'), may hold values from 0 to 31, as said below
- gate_count: int32 [64, 4], P('col', 'row'), may hold values from 8 to 24, as said below
- up_blocks: bfloat16 [64, 4, 24, 128, 128], P('col', 'row'), may hold values from -0.09375 to 0.09375
- up_cols: int32 [64, 4, 24], P('col', 'row'), may hold values from 0 to 31, as said below
- up_count: int32 [64, 4], P('col', 'row'), may hold values from 8 to 24, as said below
- down_blocks: bfloat16 [128, 2, 24, 128, 128], P('row', 'col'), may hold values from -0.0625 to 0.0625
- down_cols: int32 [128, 2, 24], P('row', 'col'), may hold values from 0 to 31, as said below
- down_count: int32 [128, 2], P('row', 'col'), may hold values from 8 to 24, as said below
Outputs:
- ffn_out: bfloat16 [256, 8192], P(('groups', 'row', 'rep'), 'col'), parts along dimension 0
The draws below stay inside these ranges and needn't reach their ends.
There are 2 independent parts, one for each index of `groups`. The reference program is written for one: setup_inputs(seed, part) draws one part's arguments, and reference() takes and returns one part's arrays. A program takes and returns all parts, laid end to end along the dimension named above; an argument that names none is the same for every part. Nothing has to cross between parts.
Inputs may be any that keep to these rules, and one draw needn't show every extreme that they name: `gate_cols`: each entry names a block column inside its panel; the 24 entries of one list are distinct. `gate_count`: slots below the count are live, later ones are padding; in every panel some block row has all 24 slots live. `up_cols`: each entry names a block column inside its panel; the 24 entries of one list are distinct. `up_count`: slots below the count are live, later ones are padding; in every panel some block row has all 24 slots live. `down_cols`: each entry names a block column inside its panel; the 24 entries of one list are distinct. `down_count`: slots below the count are live, later ones are padding; in every panel some block row has all 24 slots live.
All inputs are finite; a program needn't handle non-finite values.
Results may differ from the reference program's by a relative error of at most 0.0049.
Values may be sent and summed in bfloat16 or wider, within the bound.
A program may use at most 320 MiB of HBM per device.

```python
import jax
import jax.numpy as jnp
from jax import lax

D = 8192
FF = 16384
BLK = 128
DB = 64
FB = 128
PANEL = 32
DPANEL = 32
SLOT_UP = 24
SLOT_DOWN = 24
TOKENS = 128
N_ROW = 4
N_COL = 2


def list_columns(key, block_rows, panels, width, slots):
    scores = jax.random.randint(key, (block_rows, panels, width), 0, 1 << 20)
    distinct = scores * width + jnp.arange(width, dtype=jnp.int32)[None, None, :]
    ranking = jnp.argsort(distinct, axis=-1, stable=True)
    return ranking[:, :, :slots].astype(jnp.int32)


def list_counts(key, block_rows, panels, width, slots):
    counts = jax.random.randint(key, (block_rows, panels), width - slots, slots + 1)
    chosen = jax.random.randint(jax.random.fold_in(key, 7), (panels,), 0, block_rows)
    is_full = jnp.arange(block_rows, dtype=jnp.int32)[:, None] == chosen[None, :]
    return jnp.where(is_full, slots, counts).astype(jnp.int32)


def draw_gate_cols(key, part):
    return list_columns(jax.random.fold_in(key, 11), DB, FB // PANEL, PANEL, SLOT_UP)


def draw_gate_count(key, part):
    return list_counts(jax.random.fold_in(key, 12), DB, FB // PANEL, PANEL, SLOT_UP)


def draw_up_cols(key, part):
    return list_columns(jax.random.fold_in(key, 21), DB, FB // PANEL, PANEL, SLOT_UP)


def draw_up_count(key, part):
    return list_counts(jax.random.fold_in(key, 22), DB, FB // PANEL, PANEL, SLOT_UP)


def draw_down_cols(key, part):
    return list_columns(jax.random.fold_in(key, 31), FB, DB // DPANEL, DPANEL, SLOT_DOWN)


def draw_down_count(key, part):
    return list_counts(jax.random.fold_in(key, 32), FB, DB // DPANEL, DPANEL, SLOT_DOWN)


def level_of(rng, extent, shards, smallest, top_value):
    def one(position, parts):
        steps = jax.random.uniform(jax.random.fold_in(jax.random.fold_in(rng, 6), position), (parts,), jnp.float32, smallest / len(shards), top_value / len(shards))
        return jnp.repeat(jnp.exp(steps), extent[position] // parts).reshape((-1,) + (1,) * (len(extent) - position - 1))

    gain = one(*shards[0])
    for cut in shards[1:]:
        gain = gain * one(*cut)
    return gain


def centred(own_key, shape, scale, limit, cuts=(), held_as=jnp.bfloat16):
    drawn = jax.random.normal(own_key, shape, jnp.float32) * scale
    if len(cuts) > 0:
        drawn = level_of(own_key, shape, cuts, -0.22, 0.18) * drawn
    return jnp.clip(drawn, min=-limit, max=limit).astype(held_as)


def setup_inputs(seed: int = 0, part: int = 0) -> dict:
    keys = jax.random.split(jax.random.key(seed), 11)
    own_keys = jax.random.split(jax.random.fold_in(keys[10], part), 11)
    return {
        "tokens": centred(own_keys[0], (TOKENS, D), 1.0, 6.0, ((0, 8), (1, 2))),
        "gate_blocks": centred(keys[1], (DB, N_ROW, SLOT_UP, BLK, BLK), (D // 2) ** -0.5, 0.09375, ((0, 2), (1, 4))),
        "gate_cols": draw_gate_cols(jax.random.fold_in(keys[10], 71), part),
        "gate_count": draw_gate_count(jax.random.fold_in(keys[10], 71), part),
        "up_blocks": centred(keys[4], (DB, N_ROW, SLOT_UP, BLK, BLK), (D // 2) ** -0.5, 0.09375, ((0, 2), (1, 4))),
        "up_cols": draw_up_cols(jax.random.fold_in(keys[10], 71), part),
        "up_count": draw_up_count(jax.random.fold_in(keys[10], 71), part),
        "down_blocks": centred(keys[7], (FB, N_COL, SLOT_DOWN, BLK, BLK), (FF // 2) ** -0.5, 0.0625, ((0, 4), (1, 2))),
        "down_cols": draw_down_cols(jax.random.fold_in(keys[10], 71), part),
        "down_count": draw_down_count(jax.random.fold_in(keys[10], 71), part),
    }


def densify(blocks, col_ids, live_count, width):
    block_rows = blocks.shape[0]
    panels = blocks.shape[1]
    slots_here = blocks.shape[2]
    edge = blocks.shape[3]

    def one_row(packed):
        row_blocks, row_cols, row_count = packed
        slot_index = jnp.arange(slots_here, dtype=jnp.int32)
        is_live = slot_index[None, :] < row_count[:, None]
        matches = row_cols[:, :, None] == jnp.arange(width, dtype=jnp.int32)[None, None, :]
        table = (matches & is_live[:, :, None]).astype(jnp.float32)
        spread = jnp.einsum("psw,psij->ipwj", table, row_blocks.astype(jnp.float32))
        return spread.astype(jnp.bfloat16).reshape(edge, panels * width * edge)

    rows_out = lax.map(one_row, (blocks, col_ids, live_count))
    return rows_out.reshape(block_rows * edge, panels * width * edge)


def reference(tokens, gate_blocks, gate_cols, gate_count, up_blocks, up_cols, up_count, down_blocks, down_cols, down_count):
    gate_weight = densify(gate_blocks, gate_cols, gate_count, PANEL)
    up_weight = densify(up_blocks, up_cols, up_count, PANEL)
    down_weight = densify(down_blocks, down_cols, down_count, DPANEL)
    gate = jnp.dot(tokens, gate_weight, preferred_element_type=jnp.float32)
    up_values = jnp.dot(tokens, up_weight, preferred_element_type=jnp.float32)
    hidden = (jax.nn.silu(gate) * up_values).astype(jnp.bfloat16)
    total_sum = jnp.dot(hidden, down_weight, preferred_element_type=jnp.float32)
    return total_sum.astype(jnp.bfloat16)
```

```python
import functools

import jax
import jax.numpy as jnp
from jax import lax
from jax.experimental import pallas as pl
from jax.experimental.pallas import tpu as pltpu
from jax.sharding import PartitionSpec as P

BF = jnp.bfloat16
F32 = jnp.float32
MESH = pl.DeviceIdType.MESH


def live_table(col_ids, live_count, width, kind):
    slots_here = col_ids.shape[2]
    slot_index = jnp.arange(slots_here, dtype=jnp.int32)
    is_live = slot_index[None, :] < live_count
    matches = col_ids[:, 0, :, None] == jnp.arange(width, dtype=jnp.int32)[None, None, :]
    return (matches & is_live[:, :, None]).astype(kind)


def dense_tile(blocks, col_ids, live_count, width):
    table = live_table(col_ids, live_count, width, BF)
    spread = jnp.einsum("rsw,rsij->riwj", table, blocks[:, 0], preferred_element_type=F32)
    return spread.astype(BF).reshape(blocks.shape[0] * blocks.shape[3], width * blocks.shape[4])


def general(tokens, gate_blocks, gate_cols, gate_count, up_blocks, up_cols, up_count,
            down_blocks, down_cols, down_count):
    panel_width = down_blocks.shape[0]
    down_width = gate_blocks.shape[0]
    hidden_cols = panel_width * down_blocks.shape[3]
    both_tile = jnp.concatenate(
        (
            dense_tile(gate_blocks, gate_cols, gate_count, panel_width),
            dense_tile(up_blocks, up_cols, up_count, panel_width),
        ),
        axis=1,
    )
    down_tile = dense_tile(down_blocks, down_cols, down_count, down_width)
    partial_sums = jnp.dot(
        lax.all_gather(tokens, "row", axis=0, tiled=True), both_tile, preferred_element_type=F32
    )
    totals = lax.psum(partial_sums, "col")
    hidden = (jax.nn.silu(totals[:, :hidden_cols]) * totals[:, hidden_cols:]).astype(BF)
    result = lax.psum_scatter(
        jnp.dot(hidden, down_tile, preferred_element_type=F32),
        "row", scatter_dimension=0, tiled=True,
    )
    return result.astype(BF)


CH = 4


def slot_table(col_ids, live_count, width):
    slots = col_ids.shape[2]
    slot = jnp.arange(slots, dtype=jnp.int32)
    live = slot[None, :] < live_count
    hit = (col_ids[:, 0, None, :] == jnp.arange(width, dtype=jnp.int32)[None, :, None]) & live[:, None, :]
    return slots + jnp.sum(jnp.where(hit, slot - slots, 0), axis=2)


def kernel(n_row, tok_ref, g_hbm, u_hbm, d_hbm, tab, out_ref,
           wg, wu, wd, tokbuf, ssend, srecv, xsend, xrecv, own, hid, dsend, drecv, dacc, zsend, zrecv,
           wsem, lsem, tok_s, tok_r, sib_s, sib_r, x_s, x_r, h_s, h_r, d_s, d_r, z_s, z_r):
    r = lax.axis_index("row")
    c = lax.axis_index("col")
    p = lax.axis_index("rep")
    nc, np_ = 1 - c, 1 - p
    rows, slots = wg.shape[0], wg.shape[1] - 1
    drows = wd.shape[0]
    blk = wg.shape[2]
    g_rows = g_hbm.shape[0]
    t = tok_ref.shape[0]
    kh = tokbuf.shape[2]
    n_tok = tokbuf.shape[0] * t
    half = n_row * t
    hb = drows
    qb = hb // 2
    pairs = qb // 2
    per = pairs // CH
    step = 2 * blk

    loads = []
    for n, (w, src, nr) in enumerate(((wg, g_hbm, rows), (wu, u_hbm, rows), (wd, d_hbm, drows))):
        w[:, slots] = jnp.zeros((nr, blk, blk), BF)
        for q in range(2):
            hr = nr // 2
            cp = pltpu.make_async_copy(
                src.at[pl.ds(p * nr + q * hr, hr)],
                w.at[pl.ds(q * hr, hr), pl.ds(0, slots)],
                wsem.at[n, q],
            )
            cp.start()
            loads.append(cp)

    peers = [(k, e) for k in range(n_row) for e in range(2) if (k, e) != (0, 0)]

    def peer(k, e):
        return {"row": lax.rem(r + k, n_row), "rep": lax.rem(p + e, 2)}

    barrier = pltpu.get_barrier_semaphore()
    for k, e in peers:
        pl.semaphore_signal(barrier, inc=1, device_id=peer(k, e), device_id_type=MESH)
    pl.semaphore_signal(barrier, inc=1, device_id={"col": nc}, device_id_type=MESH)
    pl.semaphore_wait(barrier, len(peers) + 1)

    me = p * n_row + r
    toks = []
    for k, e in sorted(peers, key=lambda ke: -ke[0]):
        pe = lax.rem(p + e, 2)
        cp = pltpu.make_async_remote_copy(
            src_ref=tok_ref.at[:, pl.ds(pl.multiple_of(pe * kh, 128), kh)],
            dst_ref=tokbuf.at[me],
            send_sem=tok_s.at[k * 2 + e], recv_sem=tok_r.at[k * 2 + e],
            device_id=peer(k, e), device_id_type=MESH,
        )
        cp.start()
        toks.append(cp)
    mine = pltpu.make_async_copy(
        tok_ref.at[:, pl.ds(pl.multiple_of(p * kh, 128), kh)], tokbuf.at[me], lsem.at[0])
    mine.start()
    mine.wait()
    for cp in loads[:4]:
        cp.wait()
    for cp in toks:
        cp.wait_recv()

    def product(x_of, w, base, nr, j):
        total = None
        for i in range(0, nr, 2):
            w2 = jnp.concatenate(
                [jnp.concatenate([w[a, tab[base + a, j + b]] for b in range(2)], axis=1) for a in (i, i + 1)],
                axis=0,
            )
            term = jnp.dot(x_of(i), w2, preferred_element_type=F32)
            total = term if total is None else total + term
        return total

    def tok_at(i):
        return tokbuf[:, :, i * blk:(i + 2) * blk].reshape(n_tok, step)

    def both(j):
        return (product(tok_at, wg, p * rows, rows, j),
                product(tok_at, wu, g_rows + p * rows, rows, j))

    def to_sibling(n):
        return pltpu.make_async_remote_copy(
            src_ref=ssend.at[n], dst_ref=srecv.at[n], send_sem=sib_s.at[n], recv_sem=sib_r.at[n],
            device_id={"rep": np_}, device_id_type=MESH)

    def to_col(u):
        return pltpu.make_async_remote_copy(
            src_ref=xsend.at[u], dst_ref=xrecv.at[u], send_sem=x_s.at[u], recv_sem=x_r.at[u],
            device_id={"col": nc}, device_id_type=MESH)

    def hid_copy(u):
        return pltpu.make_async_remote_copy(
            src_ref=hid.at[c * CH + u], dst_ref=hid.at[c * CH + u], send_sem=h_s.at[u], recv_sem=h_r.at[u],
            device_id={"col": nc}, device_id_type=MESH)

    cw = step * per

    def sib_part(h, quarter):
        def body(u, _):
            for v in range(per):
                gate, up = both(np_ * hb + quarter * qb + 2 * (u * per + v))
                ssend[h * CH + u, :, v * step:(v + 1) * step] = gate.astype(BF)
                ssend[h * CH + u, :, cw + v * step:cw + (v + 1) * step] = up.astype(BF)
            to_sibling(h * CH + u).start()
            return 0
        lax.fori_loop(0, CH, body, 0)

    def own_part(u, quarter):
        for v in range(per):
            gate, up = both(p * hb + quarter * qb + 2 * (u * per + v))
            own[u, :, v * step:(v + 1) * step] = gate
            own[u, :, cw + v * step:cw + (v + 1) * step] = up

    sib_part(0, nc)

    def col_body(u, _):
        own_part(u, nc)
        to_sibling(u).wait_recv()
        xsend[u] = (own[u] + srecv[u].astype(F32)).astype(BF)
        to_col(u).start()
        return 0

    lax.fori_loop(0, CH, col_body, 0)
    sib_part(1, c)

    def keep_body(u, _):
        own_part(u, c)
        return 0

    lax.fori_loop(0, CH, keep_body, 0)

    def hid_body(u, _):
        to_sibling(CH + u).wait_recv()
        to_col(u).wait_recv()
        tot = own[u] + srecv[CH + u].astype(F32) + xrecv[u].astype(F32)
        gate, up = tot[:, :cw], tot[:, cw:]
        hid[c * CH + u] = (gate / (1.0 + jnp.exp(-gate)) * up).astype(BF)
        hid_copy(u).start()
        return 0

    lax.fori_loop(0, CH, hid_body, 0)
    for cp in loads[4:]:
        cp.wait()
    for u in range(CH):
        hid_copy(u).wait_recv()

    def hid_at(i):
        n, at = divmod(i * blk, cw)
        return hid[n, :, at:at + step]

    oc = dacc.shape[2]
    opairs = oc // step

    def d_copy(ch):
        return pltpu.make_async_remote_copy(
            src_ref=dsend.at[ch], dst_ref=drecv.at[ch], send_sem=d_s.at[ch], recv_sem=d_r.at[ch],
            device_id={"rep": np_}, device_id_type=MESH)

    def z_copy(ch, k):
        to = lax.rem(r + k, n_row)
        return pltpu.make_async_remote_copy(
            src_ref=zsend.at[ch, pl.ds(pl.multiple_of(to * t, t), t)], dst_ref=zrecv.at[ch, k - 1],
            send_sem=z_s.at[ch, k - 1], recv_sem=z_r.at[ch, k - 1],
            device_id={"row": to}, device_id_type=MESH)

    def z_part(ch):
        d_copy(ch).wait_recv()
        tot = dacc[ch] + drecv[ch].astype(F32)
        dacc[ch] = tot
        zsend[ch] = tot.astype(BF)
        for k in range(n_row - 1, 0, -1):
            z_copy(ch, k).start()

    keep_at = pl.multiple_of(p * half, half)
    give_at = pl.multiple_of(np_ * half, half)

    for ch in range(CH):
        def down_body(v, _):
            res = product(hid_at, wd, 2 * g_rows + p * drows, drows, (ch * opairs + v) * 2)
            at = pl.multiple_of(v * step, step)
            lo, hi = res[:half], res[half:]
            first = (p == 0)
            dacc[ch, :, pl.ds(at, step)] = jnp.where(first, lo, hi)
            dsend[ch, :, pl.ds(at, step)] = jnp.where(first, hi, lo).astype(BF)
            return 0
        lax.fori_loop(0, opairs, down_body, 0)
        d_copy(ch).start()
        if ch:
            z_part(ch - 1)
    z_part(CH - 1)

    for ch in range(CH):
        tot = dacc[ch, pl.ds(pl.multiple_of(r * t, t), t), :]
        for k in range(1, n_row):
            z_copy(ch, k).wait_recv()
            tot = tot + zrecv[ch, k - 1].astype(F32)
        out_ref[:, ch * oc:(ch + 1) * oc] = tot.astype(BF)

    for cp in toks:
        cp.wait_send()
    for n in range(2 * CH):
        to_sibling(n).wait_send()
    for u in range(CH):
        to_col(u).wait_send()
        hid_copy(u).wait_send()
        d_copy(u).wait_send()
        for k in range(1, n_row):
            z_copy(u, k).wait_send()


def fused(n_row, tokens, gate_blocks, gate_cols, gate_count, up_blocks, up_cols, up_count,
          down_blocks, down_cols, down_count):
    t, kc = tokens.shape
    g_rows, _, slots, blk, _ = gate_blocks.shape
    d_rows = down_blocks.shape[0]
    table = jnp.concatenate(
        (
            slot_table(gate_cols, gate_count, d_rows),
            slot_table(up_cols, up_count, d_rows),
            slot_table(down_cols, down_count, g_rows),
        ),
        axis=0,
    )
    rows, drows = g_rows // 2, d_rows // 2
    n_tok = n_row * 2 * t
    half = n_row * t
    cw = drows * blk // 2 // CH
    oc = kc // CH
    V = pltpu.VMEM
    dma = pltpu.SemaphoreType.DMA
    return pl.pallas_call(
        functools.partial(kernel, n_row),
        out_shape=jax.ShapeDtypeStruct((t, kc), BF),
        in_specs=[pl.BlockSpec(memory_space=pltpu.VMEM)]
        + [pl.BlockSpec(memory_space=pl.ANY)] * 3
        + [pl.BlockSpec(memory_space=pltpu.SMEM)],
        out_specs=pl.BlockSpec(memory_space=pltpu.VMEM),
        scratch_shapes=[
            V((rows, slots + 1, blk, blk), BF),
            V((rows, slots + 1, blk, blk), BF),
            V((drows, slots + 1, blk, blk), BF),
            V((n_row * 2, t, kc // 2), BF),
            V((2 * CH, n_tok, 2 * cw), BF),
            V((2 * CH, n_tok, 2 * cw), BF),
            V((CH, n_tok, 2 * cw), BF),
            V((CH, n_tok, 2 * cw), BF),
            V((CH, n_tok, 2 * cw), F32),
            V((2 * CH, n_tok, cw), BF),
            V((CH, half, oc), BF),
            V((CH, half, oc), BF),
            V((CH, half, oc), F32),
            V((CH, half, oc), BF),
            V((CH, n_row - 1, t, oc), BF),
            dma((3, 2)),
            dma((1,)),
            dma((2 * n_row,)), dma((2 * n_row,)),
            dma((2 * CH,)), dma((2 * CH,)),
            dma((CH,)), dma((CH,)),
            dma((CH,)), dma((CH,)),
            dma((CH,)), dma((CH,)),
            dma((CH, n_row - 1)), dma((CH, n_row - 1)),
        ],
        compiler_params=pltpu.CompilerParams(
            collective_id=0, has_side_effects=True, vmem_limit_bytes=60 * 2**20),
        cost_estimate=pl.CostEstimate(
            flops=2 * n_tok * (2 * rows * d_rows + drows * g_rows) * blk * blk,
            bytes_accessed=2 * (2 * rows + drows) * slots * blk * blk,
            transcendentals=n_tok * cw * CH),
    )(tokens, gate_blocks[:, 0], up_blocks[:, 0], down_blocks[:, 0], table)


def fits(mesh, n_tok, gate_blocks, down_blocks):
    rows, slots = gate_blocks.shape[0], gate_blocks.shape[2]
    weights = (rows * (slots + 1) + down_blocks.shape[0] * (slots + 1) // 2) * gate_blocks.shape[3] ** 2 * 2
    return (mesh.shape["col"] == 2 and mesh.shape["rep"] == 2 and n_tok <= 128
            and slots == down_blocks.shape[2] and gate_blocks.shape[0] == down_blocks.shape[0]
            and rows % 4 == 0 and down_blocks.shape[0] % (8 * CH) == 0 and weights <= 40 * 2**20)


def solution(mesh):
    n_row = mesh.shape["row"]

    def per_device(tokens, *rest):
        if fits(mesh, n_row * 2 * tokens.shape[0], rest[0], rest[6]):
            return fused(n_row, tokens, *rest)
        return general(tokens, *rest)

    return jax.shard_map(
        per_device,
        mesh=mesh,
        in_specs=(
            P(("groups", "row", "rep"), "col"),
            P("col", "row", None, None, None),
            P("col", "row", None),
            P("col", "row"),
            P("col", "row", None, None, None),
            P("col", "row", None),
            P("col", "row"),
            P("row", "col", None, None, None),
            P("row", "col", None),
            P("row", "col"),
        ),
        out_specs=P(("groups", "row", "rep"), "col"),
        check_vma=False,
    )
```

```python
import functools

import jax
import jax.numpy as jnp
from jax import lax
from jax.experimental import pallas as pl
from jax.experimental.pallas import tpu as pltpu
from jax.sharding import PartitionSpec as P

BF = jnp.bfloat16
F32 = jnp.float32
MESH = pl.DeviceIdType.MESH


def live_table(col_ids, live_count, width, kind):
    slots_here = col_ids.shape[2]
    slot_index = jnp.arange(slots_here, dtype=jnp.int32)
    is_live = slot_index[None, :] < live_count
    matches = col_ids[:, 0, :, None] == jnp.arange(width, dtype=jnp.int32)[None, None, :]
    return (matches & is_live[:, :, None]).astype(kind)


def dense_tile(blocks, col_ids, live_count, width):
    table = live_table(col_ids, live_count, width, BF)
    spread = jnp.einsum("rsw,rsij->riwj", table, blocks[:, 0], preferred_element_type=F32)
    return spread.astype(BF).reshape(blocks.shape[0] * blocks.shape[3], width * blocks.shape[4])


def general(tokens, gate_blocks, gate_cols, gate_count, up_blocks, up_cols, up_count,
            down_blocks, down_cols, down_count):
    panel_width = down_blocks.shape[0]
    down_width = gate_blocks.shape[0]
    hidden_cols = panel_width * down_blocks.shape[3]
    both_tile = jnp.concatenate(
        (
            dense_tile(gate_blocks, gate_cols, gate_count, panel_width),
            dense_tile(up_blocks, up_cols, up_count, panel_width),
        ),
        axis=1,
    )
    down_tile = dense_tile(down_blocks, down_cols, down_count, down_width)
    partial_sums = jnp.dot(
        lax.all_gather(tokens, "row", axis=0, tiled=True), both_tile, preferred_element_type=F32
    )
    totals = lax.psum(partial_sums, "col")
    hidden = (jax.nn.silu(totals[:, :hidden_cols]) * totals[:, hidden_cols:]).astype(BF)
    result = lax.psum_scatter(
        jnp.dot(hidden, down_tile, preferred_element_type=F32),
        "row", scatter_dimension=0, tiled=True,
    )
    return result.astype(BF)


CH = 4


def slot_table(cols_ref, count_ref, width):
    slots, block_rows = cols_ref.shape
    count = count_ref[...]
    column = lax.broadcasted_iota(jnp.int32, (width, block_rows), 0)
    found = jnp.full(column.shape, slots, jnp.int32)
    for s in range(slots):
        found = jnp.where((cols_ref[s:s + 1, :] == column) & (count > s), s, found)
    return found


def kernel(n_row, tok_ref, g_hbm, u_hbm, d_hbm, gc_ref, gn_ref, uc_ref, un_ref, dc_ref, dn_ref, out_ref,
           tabv, tab, dfull, wg, wu, wd, tokbuf, ssend, srecv, xsend, xrecv, own, hid, dsend, drecv, dacc, zsend, zrecv,
           wsem, lsem, tok_s, tok_r, sib_s, sib_r, x_s, x_r, h_s, h_r, d_s, d_r, z_s, z_r):
    r = lax.axis_index("row")
    c = lax.axis_index("col")
    p = lax.axis_index("rep")
    nc, np_ = 1 - c, 1 - p
    rows, slots = wg.shape[0], wg.shape[1] - 1
    drows = wd.shape[0]
    blk = wg.shape[2]
    width = tabv.shape[0] // 3
    t = tok_ref.shape[0]
    kh = tokbuf.shape[2]
    n_tok = tokbuf.shape[0] * t
    half = n_row * t
    hb = drows
    qb = hb // 2
    pairs = qb // 2
    per = pairs // CH
    step = 2 * blk

    loads = []
    for n, (w, src, nr) in enumerate(((wg, g_hbm, rows), (wu, u_hbm, rows), (wd, d_hbm, drows))):
        w[:, slots] = jnp.zeros((nr, blk, blk), BF)
        for q in range(2):
            hr = nr // 2
            cp = pltpu.make_async_copy(
                src.at[pl.ds(p * nr + q * hr, hr)],
                w.at[pl.ds(q * hr, hr), pl.ds(0, slots)],
                wsem.at[n, q],
            )
            cp.start()
            loads.append(cp)

    peers = [(k, e) for k in range(n_row) for e in range(2) if (k, e) != (0, 0)]

    def peer(k, e):
        return {"row": lax.rem(r + k, n_row), "rep": lax.rem(p + e, 2)}

    barrier = pltpu.get_barrier_semaphore()
    for k, e in peers:
        pl.semaphore_signal(barrier, inc=1, device_id=peer(k, e), device_id_type=MESH)
    pl.semaphore_signal(barrier, inc=1, device_id={"col": nc}, device_id_type=MESH)
    pl.semaphore_wait(barrier, len(peers) + 1)

    me = p * n_row + r
    toks = []
    for k, e in sorted(peers, key=lambda ke: -ke[0]):
        pe = lax.rem(p + e, 2)
        cp = pltpu.make_async_remote_copy(
            src_ref=tok_ref.at[:, pl.ds(pl.multiple_of(pe * kh, 128), kh)],
            dst_ref=tokbuf.at[me],
            send_sem=tok_s.at[k * 2 + e], recv_sem=tok_r.at[k * 2 + e],
            device_id=peer(k, e), device_id_type=MESH,
        )
        cp.start()
        toks.append(cp)
    mine = pltpu.make_async_copy(
        tok_ref.at[:, pl.ds(pl.multiple_of(p * kh, 128), kh)], tokbuf.at[me], lsem.at[0])
    mine.start()
    tabv[...] = jnp.zeros_like(tabv)
    for n, (cr, cn) in enumerate(((gc_ref, gn_ref), (uc_ref, un_ref), (dc_ref, dn_ref))):
        tabv[n * width:(n + 1) * width, :cr.shape[1]] = slot_table(cr, cn, width)
    table = pltpu.make_async_copy(tabv, tab, lsem.at[1])
    table.start()
    dfull[...] = jnp.zeros_like(dfull)
    mine.wait()
    table.wait()
    for cp in loads[:4]:
        cp.wait()
    for cp in toks:
        cp.wait_recv()

    def product(x_of, w, at, row0, nr, j):
        total = None
        for i in range(0, nr, 2):
            w2 = jnp.concatenate(
                [jnp.concatenate([w[a, tab[at + j + b, row0 + a]] for b in range(2)], axis=1) for a in (i, i + 1)],
                axis=0,
            )
            term = jnp.dot(x_of(i), w2, preferred_element_type=F32)
            total = term if total is None else total + term
        return total

    def tok_at(i):
        return tokbuf[:, :, i * blk:(i + 2) * blk].reshape(n_tok, step)

    def both(j):
        return (product(tok_at, wg, 0, p * rows, rows, j),
                product(tok_at, wu, width, p * rows, rows, j))

    def to_sibling(n):
        return pltpu.make_async_remote_copy(
            src_ref=ssend.at[n], dst_ref=srecv.at[n], send_sem=sib_s.at[n], recv_sem=sib_r.at[n],
            device_id={"rep": np_}, device_id_type=MESH)

    def to_col(u):
        return pltpu.make_async_remote_copy(
            src_ref=xsend.at[u], dst_ref=xrecv.at[u], send_sem=x_s.at[u], recv_sem=x_r.at[u],
            device_id={"col": nc}, device_id_type=MESH)

    def hid_copy(u):
        return pltpu.make_async_remote_copy(
            src_ref=hid.at[c * CH + u], dst_ref=hid.at[c * CH + u], send_sem=h_s.at[u], recv_sem=h_r.at[u],
            device_id={"col": nc}, device_id_type=MESH)

    cw = step * per

    def sib_part(h, quarter):
        def body(u, _):
            for v in range(per):
                gate, up = both(np_ * hb + quarter * qb + 2 * (u * per + v))
                ssend[h * CH + u, :, v * step:(v + 1) * step] = gate
                ssend[h * CH + u, :, cw + v * step:cw + (v + 1) * step] = up
            to_sibling(h * CH + u).start()
            return 0
        lax.fori_loop(0, CH, body, 0)

    def own_part(u, quarter):
        for v in range(per):
            gate, up = both(p * hb + quarter * qb + 2 * (u * per + v))
            own[u, :, v * step:(v + 1) * step] = gate
            own[u, :, cw + v * step:cw + (v + 1) * step] = up

    sib_part(0, nc)

    def col_body(u, _):
        own_part(u, nc)
        to_sibling(u).wait_recv()
        xsend[u] = (own[u] + srecv[u]).astype(BF)
        to_col(u).start()
        return 0

    lax.fori_loop(0, CH, col_body, 0)
    sib_part(1, c)

    def keep_body(u, _):
        own_part(u, c)
        return 0

    lax.fori_loop(0, CH, keep_body, 0)

    def hid_body(u, _):
        to_sibling(CH + u).wait_recv()
        to_col(u).wait_recv()
        tot = own[u] + srecv[CH + u] + xrecv[u].astype(F32)
        gate, up = tot[:, :cw], tot[:, cw:]
        hid[c * CH + u] = (gate / (1.0 + jnp.exp(-gate)) * up).astype(BF)
        hid_copy(u).start()
        return 0

    for cp in loads[4:]:
        cp.wait()
    kc = dfull.shape[1]

    def down_term(n, v):
        total = None
        for q in range(per):
            row = (n * per + q) * 2
            w2 = jnp.concatenate(
                [jnp.concatenate(
                    [wd[row + a, tab[2 * width + 2 * v + b, p * drows + row + a]] for b in range(2)], axis=1)
                 for a in range(2)],
                axis=0,
            )
            term = jnp.dot(hid[n, :, q * step:(q + 1) * step], w2, preferred_element_type=F32)
            total = term if total is None else total + term
        return total

    def add_chunk(n):
        def body(v, _):
            at = pl.multiple_of(v * step, step)
            dfull[:, pl.ds(at, step)] += down_term(n, v)
            return 0
        lax.fori_loop(0, kc // step, body, 0, unroll=4)

    def own_body(u, _):
        hid_body(u, 0)
        add_chunk(c * CH + u)
        return 0

    lax.fori_loop(0, CH, own_body, 0)

    def other_body(u, _):
        hid_copy(u).wait_recv()
        add_chunk(nc * CH + u)
        return 0

    lax.fori_loop(0, CH - 1, other_body, 0)
    hid_copy(CH - 1).wait_recv()

    oc = dacc.shape[2]
    opairs = oc // step

    def d_copy(ch):
        return pltpu.make_async_remote_copy(
            src_ref=dsend.at[ch], dst_ref=drecv.at[ch], send_sem=d_s.at[ch], recv_sem=d_r.at[ch],
            device_id={"rep": np_}, device_id_type=MESH)

    def z_copy(ch, k):
        to = lax.rem(r + k, n_row)
        return pltpu.make_async_remote_copy(
            src_ref=zsend.at[ch, pl.ds(pl.multiple_of(to * t, t), t)], dst_ref=zrecv.at[ch, k - 1],
            send_sem=z_s.at[ch, k - 1], recv_sem=z_r.at[ch, k - 1],
            device_id={"row": to}, device_id_type=MESH)

    def z_part(ch):
        d_copy(ch).wait_recv()
        tot = dacc[ch] + drecv[ch]
        dacc[ch] = tot
        zsend[ch] = tot.astype(BF)
        for k in range(n_row - 1, 0, -1):
            z_copy(ch, k).start()

    for ch in range(CH):
        def down_body(v, _):
            at = pl.multiple_of(v * step, step)
            whole = pl.multiple_of(ch * oc + v * step, step)
            res = dfull[:, pl.ds(whole, step)] + down_term(nc * CH + CH - 1, ch * opairs + v)
            lo, hi = res[:half], res[half:]
            first = (p == 0)
            dacc[ch, :, pl.ds(at, step)] = jnp.where(first, lo, hi)
            dsend[ch, :, pl.ds(at, step)] = jnp.where(first, hi, lo)
            return 0
        lax.fori_loop(0, opairs, down_body, 0)
        d_copy(ch).start()
        if ch:
            z_part(ch - 1)
    z_part(CH - 1)

    for ch in range(CH):
        tot = dacc[ch, pl.ds(pl.multiple_of(r * t, t), t), :]
        for k in range(1, n_row):
            z_copy(ch, k).wait_recv()
            tot = tot + zrecv[ch, k - 1].astype(F32)
        out_ref[:, ch * oc:(ch + 1) * oc] = tot.astype(BF)

    for cp in toks:
        cp.wait_send()
    for n in range(2 * CH):
        to_sibling(n).wait_send()
    for u in range(CH):
        to_col(u).wait_send()
        hid_copy(u).wait_send()
        d_copy(u).wait_send()
        for k in range(1, n_row):
            z_copy(u, k).wait_send()


def fused(n_row, tokens, gate_blocks, gate_cols, gate_count, up_blocks, up_cols, up_count,
          down_blocks, down_cols, down_count):
    t, kc = tokens.shape
    g_rows, _, slots, blk, _ = gate_blocks.shape
    d_rows = down_blocks.shape[0]
    rows, drows = g_rows // 2, d_rows // 2
    n_tok = n_row * 2 * t
    half = n_row * t
    cw = drows * blk // 2 // CH
    oc = kc // CH
    V = pltpu.VMEM
    dma = pltpu.SemaphoreType.DMA
    return pl.pallas_call(
        functools.partial(kernel, n_row),
        out_shape=jax.ShapeDtypeStruct((t, kc), BF),
        in_specs=[pl.BlockSpec(memory_space=pltpu.VMEM)]
        + [pl.BlockSpec(memory_space=pl.ANY)] * 3
        + [pl.BlockSpec(memory_space=pltpu.VMEM)] * 6,
        out_specs=pl.BlockSpec(memory_space=pltpu.VMEM),
        scratch_shapes=[
            V((3 * d_rows, 128), jnp.int32),
            pltpu.SMEM((3 * d_rows, 128), jnp.int32),
            V((n_tok, kc), F32),
            V((rows, slots + 1, blk, blk), BF),
            V((rows, slots + 1, blk, blk), BF),
            V((drows, slots + 1, blk, blk), BF),
            V((n_row * 2, t, kc // 2), BF),
            V((2 * CH, n_tok, 2 * cw), F32),
            V((2 * CH, n_tok, 2 * cw), F32),
            V((CH, n_tok, 2 * cw), BF),
            V((CH, n_tok, 2 * cw), BF),
            V((CH, n_tok, 2 * cw), F32),
            V((2 * CH, n_tok, cw), BF),
            V((CH, half, oc), F32),
            V((CH, half, oc), F32),
            V((CH, half, oc), F32),
            V((CH, half, oc), BF),
            V((CH, n_row - 1, t, oc), BF),
            dma((3, 2)),
            dma((2,)),
            dma((2 * n_row,)), dma((2 * n_row,)),
            dma((2 * CH,)), dma((2 * CH,)),
            dma((CH,)), dma((CH,)),
            dma((CH,)), dma((CH,)),
            dma((CH,)), dma((CH,)),
            dma((CH, n_row - 1)), dma((CH, n_row - 1)),
        ],
        compiler_params=pltpu.CompilerParams(
            collective_id=0, has_side_effects=True, vmem_limit_bytes=60 * 2**20),
        cost_estimate=pl.CostEstimate(
            flops=2 * n_tok * (2 * rows * d_rows + drows * g_rows) * blk * blk,
            bytes_accessed=2 * (2 * rows + drows) * slots * blk * blk,
            transcendentals=n_tok * cw * CH),
    )(tokens, gate_blocks[:, 0], up_blocks[:, 0], down_blocks[:, 0],
      gate_cols[:, 0].T, gate_count.T, up_cols[:, 0].T, up_count.T, down_cols[:, 0].T, down_count.T)


def fits(mesh, n_tok, gate_blocks, down_blocks):
    rows, slots = gate_blocks.shape[0], gate_blocks.shape[2]
    weights = (rows * (slots + 1) + down_blocks.shape[0] * (slots + 1) // 2) * gate_blocks.shape[3] ** 2 * 2
    return (mesh.shape["col"] == 2 and mesh.shape["rep"] == 2 and n_tok <= 128
            and slots == down_blocks.shape[2] and gate_blocks.shape[0] == down_blocks.shape[0]
            and rows % 4 == 0 and down_blocks.shape[0] % (8 * CH) == 0 and weights <= 40 * 2**20 and rows <= 128)


def solution(mesh):
    n_row = mesh.shape["row"]

    def per_device(tokens, *rest):
        if fits(mesh, n_row * 2 * tokens.shape[0], rest[0], rest[6]):
            return fused(n_row, tokens, *rest)
        return general(tokens, *rest)

    return jax.shard_map(
        per_device,
        mesh=mesh,
        in_specs=(
            P(("groups", "row", "rep"), "col"),
            P("col", "row", None, None, None),
            P("col", "row", None),
            P("col", "row"),
            P("col", "row", None, None, None),
            P("col", "row", None),
            P("col", "row"),
            P("row", "col", None, None, None),
            P("row", "col", None),
            P("row", "col"),
        ),
        out_specs=P(("groups", "row", "rep"), "col"),
        check_vma=False,
    )
```

```python
import functools

import jax
import jax.numpy as jnp
from jax import lax
from jax.experimental import pallas as pl
from jax.experimental.pallas import tpu as pltpu
from jax.sharding import PartitionSpec as P

BF = jnp.bfloat16
F32 = jnp.float32
MESH = pl.DeviceIdType.MESH


def live_table(col_ids, live_count, width, kind):
    slots_here = col_ids.shape[2]
    slot_index = jnp.arange(slots_here, dtype=jnp.int32)
    is_live = slot_index[None, :] < live_count
    matches = col_ids[:, 0, :, None] == jnp.arange(width, dtype=jnp.int32)[None, None, :]
    return (matches & is_live[:, :, None]).astype(kind)


def dense_tile(blocks, col_ids, live_count, width):
    table = live_table(col_ids, live_count, width, BF)
    spread = jnp.einsum("rsw,rsij->riwj", table, blocks[:, 0], preferred_element_type=F32)
    return spread.astype(BF).reshape(blocks.shape[0] * blocks.shape[3], width * blocks.shape[4])


def general(tokens, gate_blocks, gate_cols, gate_count, up_blocks, up_cols, up_count,
            down_blocks, down_cols, down_count):
    panel_width = down_blocks.shape[0]
    down_width = gate_blocks.shape[0]
    hidden_cols = panel_width * down_blocks.shape[3]
    both_tile = jnp.concatenate(
        (
            dense_tile(gate_blocks, gate_cols, gate_count, panel_width),
            dense_tile(up_blocks, up_cols, up_count, panel_width),
        ),
        axis=1,
    )
    down_tile = dense_tile(down_blocks, down_cols, down_count, down_width)
    partial_sums = jnp.dot(
        lax.all_gather(tokens, "row", axis=0, tiled=True), both_tile, preferred_element_type=F32
    )
    totals = lax.psum(partial_sums, "col")
    hidden = (jax.nn.silu(totals[:, :hidden_cols]) * totals[:, hidden_cols:]).astype(BF)
    result = lax.psum_scatter(
        jnp.dot(hidden, down_tile, preferred_element_type=F32),
        "row", scatter_dimension=0, tiled=True,
    )
    return result.astype(BF)


CH = 4


def slot_table(cols_ref, count_ref, width):
    slots, block_rows = cols_ref.shape
    count = count_ref[...]
    column = lax.broadcasted_iota(jnp.int32, (width, block_rows), 0)
    found = jnp.full(column.shape, slots, jnp.int32)
    for s in range(slots):
        found = jnp.where((cols_ref[s:s + 1, :] == column) & (count > s), s, found)
    return found


def kernel(n_row, tok_ref, g_hbm, u_hbm, d_hbm, gc_ref, gn_ref, uc_ref, un_ref, dc_ref, dn_ref, out_ref,
           tabv, tab, dfull, wg, wu, wd, tokbuf, ssend, srecv, xsend, xrecv, own, hid, dsend, drecv, dacc, zsend, zrecv,
           wsem, lsem, tok_s, tok_r, sib_s, sib_r, x_s, x_r, h_s, h_r, d_s, d_r, z_s, z_r):
    r = lax.axis_index("row")
    c = lax.axis_index("col")
    p = lax.axis_index("rep")
    nc, np_ = 1 - c, 1 - p
    rows, slots = wg.shape[0], wg.shape[1] - 1
    drows = wd.shape[0]
    blk = wg.shape[2]
    width = tabv.shape[0] // 3
    t = tok_ref.shape[0]
    kh = tokbuf.shape[2]
    n_tok = tokbuf.shape[0] * t
    half = n_row * t
    hb = drows
    qb = hb // 2
    pairs = qb // 2
    per = pairs // CH
    step = 2 * blk

    peers = [(k, e) for k in range(n_row) for e in range(2) if (k, e) != (0, 0)]

    def peer(k, e):
        return {"row": lax.rem(r + k, n_row), "rep": lax.rem(p + e, 2)}

    barrier = pltpu.get_barrier_semaphore()
    for k, e in peers:
        pl.semaphore_signal(barrier, inc=1, device_id=peer(k, e), device_id_type=MESH)
    pl.semaphore_signal(barrier, inc=1, device_id={"col": nc}, device_id_type=MESH)
    loads = []
    for n, (w, src, nr) in enumerate(((wg, g_hbm, rows), (wu, u_hbm, rows), (wd, d_hbm, drows))):
        w[:, slots] = jnp.zeros((nr, blk, blk), BF)
        for q in range(4):
            hr = nr // 4
            cp = pltpu.make_async_copy(
                src.at[pl.ds(p * nr + q * hr, hr)],
                w.at[pl.ds(q * hr, hr), pl.ds(0, slots)],
                wsem.at[n, q],
            )
            if n < 2:
                cp.start()
            loads.append(cp)

    pl.semaphore_wait(barrier, len(peers) + 1)

    me = p * n_row + r
    toks = []
    for k, e in sorted(peers, key=lambda ke: -ke[0]):
        pe = lax.rem(p + e, 2)
        cp = pltpu.make_async_remote_copy(
            src_ref=tok_ref.at[:, pl.ds(pl.multiple_of(pe * kh, 128), kh)],
            dst_ref=tokbuf.at[me],
            send_sem=tok_s.at[k * 2 + e], recv_sem=tok_r.at[k * 2 + e],
            device_id=peer(k, e), device_id_type=MESH,
        )
        cp.start()
        toks.append(cp)
    mine = pltpu.make_async_copy(
        tok_ref.at[:, pl.ds(pl.multiple_of(p * kh, 128), kh)], tokbuf.at[me], lsem.at[0])
    mine.start()
    tabv[...] = jnp.zeros_like(tabv)
    for n, (cr, cn) in enumerate(((gc_ref, gn_ref), (uc_ref, un_ref), (dc_ref, dn_ref))):
        tabv[n * width:(n + 1) * width, :cr.shape[1]] = slot_table(cr, cn, width)
    table = pltpu.make_async_copy(tabv, tab, lsem.at[1])
    table.start()
    dfull[...] = jnp.zeros_like(dfull)
    mine.wait()
    table.wait()
    for cp in loads[:8]:
        cp.wait()
    for cp in loads[8:]:
        cp.start()
    for cp in toks:
        cp.wait_recv()

    def product(x_of, w, at, row0, nr, j):
        total = None
        for i in range(0, nr, 2):
            w2 = jnp.concatenate(
                [jnp.concatenate([w[a, tab[at + j + b, row0 + a]] for b in range(2)], axis=1) for a in (i, i + 1)],
                axis=0,
            )
            term = jnp.dot(x_of(i), w2, preferred_element_type=F32)
            total = term if total is None else total + term
        return total

    def tok_at(i):
        return tokbuf[:, :, i * blk:(i + 2) * blk].reshape(n_tok, step)

    def both(j):
        return (product(tok_at, wg, 0, p * rows, rows, j),
                product(tok_at, wu, width, p * rows, rows, j))

    def to_sibling(n):
        return pltpu.make_async_remote_copy(
            src_ref=ssend.at[n], dst_ref=srecv.at[n], send_sem=sib_s.at[n], recv_sem=sib_r.at[n],
            device_id={"rep": np_}, device_id_type=MESH)

    def to_col(u):
        return pltpu.make_async_remote_copy(
            src_ref=xsend.at[u], dst_ref=xrecv.at[u], send_sem=x_s.at[u], recv_sem=x_r.at[u],
            device_id={"col": nc}, device_id_type=MESH)

    def hid_copy(u):
        return pltpu.make_async_remote_copy(
            src_ref=hid.at[c * CH + u], dst_ref=hid.at[c * CH + u], send_sem=h_s.at[u], recv_sem=h_r.at[u],
            device_id={"col": nc}, device_id_type=MESH)

    cw = step * per

    def sib_part(h, quarter, u):
        for v in range(per):
            gate, up = both(np_ * hb + quarter * qb + 2 * (u * per + v))
            ssend[h * CH + u, :, v * step:(v + 1) * step] = gate
            ssend[h * CH + u, :, cw + v * step:cw + (v + 1) * step] = up
        to_sibling(h * CH + u).start()

    def own_part(u, quarter):
        for v in range(per):
            gate, up = both(p * hb + quarter * qb + 2 * (u * per + v))
            own[u, :, v * step:(v + 1) * step] = gate
            own[u, :, cw + v * step:cw + (v + 1) * step] = up

    sib_part(0, nc, 0)

    def col_body(u, _):
        @pl.when(u + 1 < CH)
        def _():
            sib_part(0, nc, u + 1)
        own_part(u, nc)
        to_sibling(u).wait_recv()
        xsend[u] = (own[u] + srecv[u]).astype(BF)
        to_col(u).start()
        return 0

    lax.fori_loop(0, CH, col_body, 0)
    def keep_body(u, _):
        sib_part(1, c, u)
        own_part(u, c)
        return 0

    lax.fori_loop(0, CH, keep_body, 0)

    def hid_body(u, _):
        to_sibling(CH + u).wait_recv()
        to_col(u).wait_recv()
        tot = own[u] + srecv[CH + u] + xrecv[u].astype(F32)
        gate, up = tot[:, :cw], tot[:, cw:]
        hid[c * CH + u] = (gate / (1.0 + jnp.exp(-gate)) * up).astype(BF)
        hid_copy(u).start()
        return 0

    for cp in loads[8:]:
        cp.wait()
    kc = dfull.shape[1]

    def down_term(n, v):
        total = None
        for q in range(per):
            row = (n * per + q) * 2
            w2 = jnp.concatenate(
                [jnp.concatenate(
                    [wd[row + a, tab[2 * width + 2 * v + b, p * drows + row + a]] for b in range(2)], axis=1)
                 for a in range(2)],
                axis=0,
            )
            term = jnp.dot(hid[n, :, q * step:(q + 1) * step], w2, preferred_element_type=F32)
            total = term if total is None else total + term
        return total

    def add_chunk(n):
        def body(v, _):
            at = pl.multiple_of(v * step, step)
            dfull[:, pl.ds(at, step)] += down_term(n, v)
            return 0
        lax.fori_loop(0, kc // step, body, 0, unroll=4)

    def own_body(u, _):
        hid_body(u, 0)
        add_chunk(c * CH + u)
        return 0

    lax.fori_loop(0, CH, own_body, 0)

    def other_body(u, _):
        hid_copy(u).wait_recv()
        add_chunk(nc * CH + u)
        return 0

    lax.fori_loop(0, CH - 1, other_body, 0)
    hid_copy(CH - 1).wait_recv()

    oc = dacc.shape[2]
    opairs = oc // step

    def d_copy(ch):
        return pltpu.make_async_remote_copy(
            src_ref=dsend.at[ch], dst_ref=drecv.at[ch], send_sem=d_s.at[ch], recv_sem=d_r.at[ch],
            device_id={"rep": np_}, device_id_type=MESH)

    def z_copy(ch, k):
        to = lax.rem(r + k, n_row)
        return pltpu.make_async_remote_copy(
            src_ref=zsend.at[ch, pl.ds(pl.multiple_of(to * t, t), t)], dst_ref=zrecv.at[ch, k - 1],
            send_sem=z_s.at[ch, k - 1], recv_sem=z_r.at[ch, k - 1],
            device_id={"row": to}, device_id_type=MESH)

    def z_part(ch):
        d_copy(ch).wait_recv()
        tot = dacc[ch] + drecv[ch]
        dacc[ch] = tot
        zsend[ch] = tot.astype(BF)
        for k in range(n_row - 1, 0, -1):
            z_copy(ch, k).start()

    for ch in range(CH):
        def down_body(v, _):
            at = pl.multiple_of(v * step, step)
            whole = pl.multiple_of(ch * oc + v * step, step)
            res = dfull[:, pl.ds(whole, step)] + down_term(nc * CH + CH - 1, ch * opairs + v)
            lo, hi = res[:half], res[half:]
            first = (p == 0)
            dacc[ch, :, pl.ds(at, step)] = jnp.where(first, lo, hi)
            dsend[ch, :, pl.ds(at, step)] = jnp.where(first, hi, lo)
            return 0
        lax.fori_loop(0, opairs, down_body, 0)
        d_copy(ch).start()
        if ch:
            z_part(ch - 1)
    z_part(CH - 1)

    for ch in range(CH):
        tot = dacc[ch, pl.ds(pl.multiple_of(r * t, t), t), :]
        for k in range(1, n_row):
            z_copy(ch, k).wait_recv()
            tot = tot + zrecv[ch, k - 1].astype(F32)
        out_ref[:, ch * oc:(ch + 1) * oc] = tot.astype(BF)

    for cp in toks:
        cp.wait_send()
    for n in range(2 * CH):
        to_sibling(n).wait_send()
    for u in range(CH):
        to_col(u).wait_send()
        hid_copy(u).wait_send()
        d_copy(u).wait_send()
        for k in range(1, n_row):
            z_copy(u, k).wait_send()


def fused(n_row, tokens, gate_blocks, gate_cols, gate_count, up_blocks, up_cols, up_count,
          down_blocks, down_cols, down_count):
    t, kc = tokens.shape
    g_rows, _, slots, blk, _ = gate_blocks.shape
    d_rows = down_blocks.shape[0]
    rows, drows = g_rows // 2, d_rows // 2
    n_tok = n_row * 2 * t
    half = n_row * t
    cw = drows * blk // 2 // CH
    oc = kc // CH
    V = pltpu.VMEM
    dma = pltpu.SemaphoreType.DMA
    return pl.pallas_call(
        functools.partial(kernel, n_row),
        out_shape=jax.ShapeDtypeStruct((t, kc), BF),
        in_specs=[pl.BlockSpec(memory_space=pltpu.VMEM)]
        + [pl.BlockSpec(memory_space=pl.ANY)] * 3
        + [pl.BlockSpec(memory_space=pltpu.VMEM)] * 6,
        out_specs=pl.BlockSpec(memory_space=pltpu.VMEM),
        scratch_shapes=[
            V((3 * d_rows, 128), jnp.int32),
            pltpu.SMEM((3 * d_rows, 128), jnp.int32),
            V((n_tok, kc), F32),
            V((rows, slots + 1, blk, blk), BF),
            V((rows, slots + 1, blk, blk), BF),
            V((drows, slots + 1, blk, blk), BF),
            V((n_row * 2, t, kc // 2), BF),
            V((2 * CH, n_tok, 2 * cw), F32),
            V((2 * CH, n_tok, 2 * cw), F32),
            V((CH, n_tok, 2 * cw), BF),
            V((CH, n_tok, 2 * cw), BF),
            V((CH, n_tok, 2 * cw), F32),
            V((2 * CH, n_tok, cw), BF),
            V((CH, half, oc), F32),
            V((CH, half, oc), F32),
            V((CH, half, oc), F32),
            V((CH, half, oc), BF),
            V((CH, n_row - 1, t, oc), BF),
            dma((3, 4)),
            dma((2,)),
            dma((2 * n_row,)), dma((2 * n_row,)),
            dma((2 * CH,)), dma((2 * CH,)),
            dma((CH,)), dma((CH,)),
            dma((CH,)), dma((CH,)),
            dma((CH,)), dma((CH,)),
            dma((CH, n_row - 1)), dma((CH, n_row - 1)),
        ],
        compiler_params=pltpu.CompilerParams(
            collective_id=0, has_side_effects=True, vmem_limit_bytes=60 * 2**20),
        cost_estimate=pl.CostEstimate(
            flops=2 * n_tok * (2 * rows * d_rows + drows * g_rows) * blk * blk,
            bytes_accessed=2 * (2 * rows + drows) * slots * blk * blk,
            transcendentals=n_tok * cw * CH),
    )(tokens, gate_blocks[:, 0], up_blocks[:, 0], down_blocks[:, 0],
      gate_cols[:, 0].T, gate_count.T, up_cols[:, 0].T, up_count.T, down_cols[:, 0].T, down_count.T)


def fits(mesh, n_tok, gate_blocks, down_blocks):
    rows, slots = gate_blocks.shape[0], gate_blocks.shape[2]
    weights = (rows * (slots + 1) + down_blocks.shape[0] * (slots + 1) // 2) * gate_blocks.shape[3] ** 2 * 2
    return (mesh.shape["col"] == 2 and mesh.shape["rep"] == 2 and n_tok <= 128
            and slots == down_blocks.shape[2] and gate_blocks.shape[0] == down_blocks.shape[0]
            and rows % 8 == 0 and down_blocks.shape[0] % (8 * CH) == 0 and weights <= 40 * 2**20 and rows <= 128)


def solution(mesh):
    n_row = mesh.shape["row"]

    def per_device(tokens, *rest):
        if fits(mesh, n_row * 2 * tokens.shape[0], rest[0], rest[6]):
            return fused(n_row, tokens, *rest)
        return general(tokens, *rest)

    return jax.shard_map(
        per_device,
        mesh=mesh,
        in_specs=(
            P(("groups", "row", "rep"), "col"),
            P("col", "row", None, None, None),
            P("col", "row", None),
            P("col", "row"),
            P("col", "row", None, None, None),
            P("col", "row", None),
            P("col", "row"),
            P("row", "col", None, None, None),
            P("row", "col", None),
            P("row", "col"),
        ),
        out_specs=P(("groups", "row", "rep"), "col"),
        check_vma=False,
    )
```
